512 devices in a mesh: az: 16 (over x, z_lo, core), lat: 8 (over y), ta: 4 (over z_hi).
Axes of the slice: x: 4, y: 8, z: 8 (z_hi: 4, z_lo: 2; z = z_hi * 2 + z_lo), core: 2. Of those that a mesh axis runs over, the one named last changes fastest.
Arguments:
- queries: bfloat16 [4, 128, 256, 1024], P('ta', 'lat', 'az'), may hold values from -8 to 8
- keys_values: bfloat16 [2, 4, 128, 256, 1024], P(None, 'ta', 'lat', 'az'), may hold values from -8 to 8
- windows: int32 [4, 16, 32, 15], P('ta', 'lat', 'az'), may hold values from -1 to 2047, as said below
Outputs:
- attended: bfloat16 [4, 128, 256, 1024], P('ta', 'lat', 'az')
The draws below stay inside these ranges and needn't reach their ends.
Inputs may be any that keep to these rules, and one draw needn't show every extreme that they name: Each row windows[f, r, c] lists distinct tiles, the tile (f, r, c) among them; every other listed tile is in frame f and at most two tile columns away around the azimuth loop in tile row r, or at most two tile rows away in tile column c, or at most one tile row and one tile column away, or it is tile (f - 1, r, c) or (f + 1, r, c). Tile rows never wrap across the poles. -1 marks an empty slot.
All inputs are finite; a program needn't handle non-finite values.
Results may differ from the reference program's by a relative error of at most 0.0027.
Values may be sent and summed in bfloat16 or wider, within the bound.
A program may use at most 64 MiB of HBM per device.

```python
import math
import jax
import jax.numpy as jnp
from jax import lax

HEADS = 8
HD = 128
TS = 8
WMAX = 15
HF = 1024
FRAMES = 4
NLAT = 128
NAZ = 256
TRA = 16
TCA = 32


def draw_queries(key, part):
    key = jax.random.fold_in(key, 11)
    full_shape = (FRAMES, NLAT, NAZ, HF)
    base_field = jnp.clip(2.0 * jax.random.normal(key, full_shape), -6.0, 6.0)
    return base_field.astype(jnp.bfloat16)


def draw_keys_values(key, part):
    key = jax.random.fold_in(key, 12)
    full_shape = (FRAMES, NLAT, NAZ, HF)
    key_draw, value_draw, scale_draw = jax.random.split(key, 3)
    row_scale = jnp.exp(jax.random.uniform(scale_draw, (FRAMES, NLAT, NAZ, 1), minval=math.log(0.5), maxval=math.log(2.0)))
    key_field = jnp.clip(jax.random.normal(key_draw, full_shape), -4.0, 4.0) * row_scale
    value_field = jnp.clip(jax.random.normal(value_draw, full_shape), -4.0, 4.0)
    return jnp.stack([key_field, value_field], axis=0).astype(jnp.bfloat16)


def draw_windows(key, part):
    key = jax.random.fold_in(key, 13)
    grid_shape = (FRAMES, TRA, TCA)
    frame_grid = jnp.broadcast_to(jnp.arange(FRAMES)[:, None, None], grid_shape)
    row_grid = jnp.broadcast_to(jnp.arange(TRA)[None, :, None], grid_shape)
    col_grid = jnp.broadcast_to(jnp.arange(TCA)[None, None, :], grid_shape)
    polar = (row_grid < TRA // 4) | (row_grid >= TRA - TRA // 4)
    coin_keys = jax.random.split(key, WMAX + 1)
    offsets = []
    for row_step in (-1, 0, 1):
        for col_step in (-1, 0, 1):
            offsets.append((0, row_step, col_step, True))
    offsets.append((0, 0, -2, False))
    offsets.append((0, 0, 2, False))
    offsets.append((0, -2, 0, False))
    offsets.append((0, 2, 0, False))
    offsets.append((-1, 0, 0, False))
    offsets.append((1, 0, 0, False))
    listed = []
    for slot_index in range(WMAX):
        frame_step, row_step, col_step, always = offsets[slot_index]
        new_frame = frame_grid + frame_step
        new_row = row_grid + row_step
        new_col = (col_grid + col_step) % TCA
        inside = (new_frame >= 0) & (new_frame < FRAMES) & (new_row >= 0) & (new_row < TRA)
        coin_flip = jax.random.randint(coin_keys[slot_index], grid_shape, 0, 4) < 3
        if always:
            keep = inside
        elif frame_step != 0:
            keep = inside & coin_flip
        else:
            keep = inside & polar & coin_flip
        tile_number = (new_frame * TRA + new_row) * TCA + new_col
        listed.append(jnp.where(keep, tile_number, -1))
    stacked = jnp.stack(listed, axis=-1)
    order_scores = jax.random.randint(coin_keys[WMAX], grid_shape + (WMAX,), 0, 1 << 20) * 32 + jnp.arange(WMAX)
    axis_order = jnp.argsort(order_scores, axis=-1, stable=True)
    return jnp.take_along_axis(stacked, axis_order, axis=-1).astype(jnp.int32)


def setup_inputs(seed: int = 0) -> dict:
    seeds = jax.random.split(jax.random.key(seed), 4)
    return {
        "queries": draw_queries(jax.random.fold_in(seeds[3], 71), 0),
        "keys_values": draw_keys_values(jax.random.fold_in(seeds[3], 71), 0),
        "windows": draw_windows(jax.random.fold_in(seeds[3], 71), 0),
    }


def to_tiles(field):
    frame_count, row_count, col_count, channels = field.shape
    shaped = field.reshape(frame_count, row_count // TS, TS, col_count // TS, TS, channels)
    return shaped.transpose(0, 1, 3, 2, 4, 5).reshape(-1, TS * TS, channels)

def from_tiles(tile_set, frame_count, row_count, col_count):
    channels = tile_set.shape[-1]
    shaped = tile_set.reshape(frame_count, row_count // TS, col_count // TS, TS, TS, channels)
    return shaped.transpose(0, 1, 3, 2, 4, 5).reshape(frame_count, row_count, col_count, channels)

def reference(queries, keys_values, windows):
    tokens = TS * TS
    query_tiles = to_tiles(queries)
    key_tiles = to_tiles(keys_values[0])
    value_tiles = to_tiles(keys_values[1])
    query_rows = query_tiles.reshape(-1, TCA, tokens, HF)
    window_rows = windows.reshape(-1, TCA, WMAX)
    score_scale = 1.0 / math.sqrt(HD)

    def attend_row(row_item):
        query_block, listed = row_item
        clamped = jnp.maximum(listed, 0).astype(jnp.int32)
        key_block = key_tiles[clamped].reshape(TCA, WMAX * tokens, HEADS, HD).astype(jnp.float32)
        value_block = value_tiles[clamped].reshape(TCA, WMAX * tokens, HEADS, HD).astype(jnp.float32)
        query_float = query_block.reshape(TCA, tokens, HEADS, HD).astype(jnp.float32)
        scores = jnp.einsum('tqhd,tkhd->thqk', query_float, key_block, precision=lax.Precision.HIGHEST) * score_scale
        filled = jnp.repeat(listed >= 0, tokens, axis=1)
        scores = jnp.where(filled[:, None, None, :], scores, -jnp.inf)
        peak_score = lax.optimization_barrier(jnp.max(scores, axis=-1, keepdims=True))
        weights = jnp.exp(scores - peak_score)
        weight_sum = lax.optimization_barrier(jnp.sum(weights, axis=-1, keepdims=True))
        rounded = lax.optimization_barrier(weights.astype(jnp.bfloat16)).astype(jnp.float32)
        summed = jnp.einsum('thqk,tkhd->thqd', rounded, value_block, precision=lax.Precision.HIGHEST)
        result = (summed / weight_sum).transpose(0, 2, 1, 3).reshape(TCA, tokens, HF)
        return result.astype(jnp.bfloat16)
    attended = lax.map(attend_row, (query_rows, window_rows))
    return from_tiles(attended.reshape(-1, tokens, HF), FRAMES, NLAT, NAZ)
```

```python
import functools
import math

import jax
import jax.numpy as jnp
from jax import lax
from jax.experimental import pallas as pl
from jax.experimental.pallas import tpu as pltpu
from jax.sharding import PartitionSpec as P

MESH = pl.DeviceIdType.MESH
HD = 128
TS = 8
ROWS, COLS = 16, 16
PAIR = TS * COLS
NEG = -1e30

OWN, CORE, CROSS, XREL, TDIR, TREL, UP, DOWN = range(8)
CORNER_UP, CORNER_DOWN = 8, 9
TRANSFERS = (CORE, CROSS, XREL, TDIR, TREL, UP, DOWN, CORNER_UP, CORNER_DOWN)
KEYS, VALUES = 0, 1
CHUNKS = [(kind, half) for kind in (KEYS, VALUES) for half in (0, 1)]

CORNER = 8
PLACES = [
    {
        (OWN, 0): 0, (OWN, 1): 1, (CORE, 0): 2, (CORE, 1): 3, (XREL, 0): 4, (XREL, 1): 5,
        (UP, 0): 6, (UP, 1): 7, (DOWN, 0): 8, (CORNER, 0): 9, (TREL, 0): 10, (TDIR, 0): 11,
    },
    {
        (OWN, 0): 0, (OWN, 1): 1, (CORE, 0): 2, (CORE, 1): 3, (XREL, 0): 4, (XREL, 1): 5,
        (UP, 1): 6, (DOWN, 0): 7, (DOWN, 1): 8, (CORNER, 1): 9, (TREL, 1): 10, (TDIR, 1): 11,
    },
]
NPLACE = 12


def when(condition, action):
    if condition is None:
        action()
    else:
        pl.when(condition)(action)


def kernel(
    heads, n_az, n_lat, n_ta, windows, q_hbm, kv_hbm, out_hbm,
    blocks, corner, corner_out, q, bias, scores, weights, peak, total, acc, out,
    send_sem, recv_sem, local_sem,
):
    az, lat, ta = lax.axis_index("az"), lax.axis_index("lat"), lax.axis_index("ta")
    place4 = lax.rem(az, 4)
    core = lax.rem(az, 2)
    cross = az + 3 - 2 * place4
    step = jnp.where(place4 >= 2, 1, -1)
    x_step = jnp.where(place4 == 3, -4, 4)
    outer = (place4 == 0) | (place4 == 3)
    frame_ok = lambda f: (f >= 0) & (f < n_ta)
    at = lambda a, l, t: {"az": a, "lat": l, "ta": t}
    routes = {
        CORE: (at(az + 1 - 2 * core, lat, ta),) * 2 + (None, None),
        CROSS: (at(cross, lat, ta),) * 2 + (None, None),
        XREL: (
            at(lax.rem(az + x_step + n_az, n_az), lat, ta),
            at(lax.rem(az - x_step + n_az, n_az), lat, ta),
            outer, outer,
        ),
        TDIR: (at(az, lat, ta + step), at(az, lat, ta - step), frame_ok(ta + step), frame_ok(ta - step)),
        TREL: (at(cross, lat, ta + step),) * 2 + (frame_ok(ta + step),) * 2,
        UP: (at(az, lat + 1, ta), at(az, lat - 1, ta), lat < n_lat - 1, lat > 0),
        DOWN: (at(az, lat - 1, ta), at(az, lat + 1, ta), lat > 0, lat < n_lat - 1),
    }
    routes[CORNER_UP] = routes[UP]
    routes[CORNER_DOWN] = routes[DOWN]

    barrier = pltpu.get_barrier_semaphore()
    count = 0
    for name in (CORE, CROSS, XREL, TDIR, TREL, UP, DOWN):
        _, source, sends, receives = routes[name]
        when(receives, functools.partial(
            pl.semaphore_signal, barrier, inc=1, device_id=source, device_id_type=MESH))
        count = count + (1 if sends is None else sends.astype(jnp.int32))
    pl.semaphore_wait(barrier, count)

    def rows(half):
        return pl.ds(half * TS, TS)

    def copy(name, kind, half):
        slot = TRANSFERS.index(name)
        chunk = 2 * kind + half
        if name in (CORNER_UP, CORNER_DOWN):
            source = corner_out.at[name - CORNER_UP, kind]
            target = corner.at[name - CORNER_UP, kind]
        else:
            target = blocks.at[name, kind, rows(half)]
            if name in (XREL, TREL):
                source = blocks.at[CROSS, kind, rows(half)]
            else:
                source = kv_hbm.at[kind, 0, rows(half)]
        return pltpu.make_async_remote_copy(
            src_ref=source, dst_ref=target,
            send_sem=send_sem.at[slot, chunk], recv_sem=recv_sem.at[slot, chunk],
            device_id=routes[name][0], device_id_type=MESH,
        )

    started = []

    def start(name, kind, halves=(0, 1)):
        for half in halves:
            started.append((name, kind, half))
            when(routes[name][2], copy(name, kind, half).start)

    def arrived(name, kind, halves=(0, 1)):
        for half in halves:
            when(routes[name][3], copy(name, kind, half).wait_recv)

    def relay(kind, half):
        arrived(CROSS, kind, (half,))
        start(XREL, kind, (half,))
        start(TREL, kind, (half,))

    start(CROSS, KEYS)
    start(TDIR, KEYS)
    start(UP, KEYS)
    start(DOWN, KEYS)
    start(CORE, KEYS)
    get_q = pltpu.make_async_copy(q_hbm.at[0], q, local_sem.at[0])
    get_k = pltpu.make_async_copy(kv_hbm.at[KEYS, 0], blocks.at[OWN, KEYS], local_sem.at[1])
    get_v = pltpu.make_async_copy(kv_hbm.at[VALUES, 0], blocks.at[OWN, VALUES], local_sem.at[2])
    get_q.start()
    get_k.start()
    get_v.start()
    start(CROSS, VALUES)
    start(CORE, VALUES)
    start(UP, VALUES)
    start(DOWN, VALUES)

    def clear(name):
        def body():
            blocks[name] = jnp.zeros(blocks.shape[1:], blocks.dtype)
        return body

    def clear_corner(index):
        def body():
            corner[index] = jnp.zeros(corner.shape[1:], corner.dtype)
        return body

    for name in (TDIR, TREL, UP, DOWN):
        when(jnp.logical_not(routes[name][3]), clear(name))
    when(lat == 0, clear_corner(0))
    when(lat == n_lat - 1, clear_corner(1))

    rows_all, cols_all = 2 * n_lat, 2 * n_az
    lane = lax.broadcasted_iota(jnp.int32, (8, PAIR), 1)
    right_tile = lax.rem(lane // TS, 2)
    col_on = jnp.where(core == 0, 2, -2)
    for r in range(2):
        tiles = [None] * NPLACE
        for (name, half), place in PLACES[r].items():
            frame, row, col = ta, half, right_tile
            if name == CORE:
                col = col + col_on
            elif name == XREL:
                col = col - col_on
            elif name == UP:
                row = half - 2
            elif name == DOWN:
                row = half + 2
            elif name == CORNER:
                row = 3 * half - 1
                col = jnp.where(right_tile == 0, 2, -1)
            elif name == TDIR:
                frame = ta - step
            elif name == TREL:
                frame = ta + step
            row = row + 2 * lat
            there = (row >= 0) & (row < rows_all) & (frame >= 0) & (frame < n_ta)
            first = jnp.where(there, (frame * rows_all + row) * cols_all, -4 * cols_all)
            tiles[place] = first + lax.rem(col + 2 * az + cols_all, cols_all)
        tiles = jnp.stack(tiles, axis=0)
        for c in range(2):
            listed = tiles == windows[0, r, c, 0]
            for slot in range(1, windows.shape[3]):
                listed = listed | (tiles == windows[0, r, c, slot])
            bias[r, :, c * 8:(c + 1) * 8, :] = jnp.where(listed, 0.0, NEG)

    off = jnp.where(outer, XREL, CROSS)
    scale = 1.0 / math.sqrt(HD)

    def key_block(name, half, kind, columns):
        if name == CORNER:
            block = corner[half, kind, :, :, columns]
        else:
            block = blocks[off if name == XREL else name, kind, rows(half), :, columns]
        return block.reshape(PAIR, HD)

    def add_keys(*names, first=False):
        def head(h, carry):
            columns = pl.ds(pl.multiple_of(h * HD, HD), HD)
            for r in range(2):
                query = q[rows(r), :, columns].reshape(PAIR, HD)
                best = None if first else peak[r, h]
                for (name, half), place in PLACES[r].items():
                    if name not in names:
                        continue
                    score = lax.dot_general(
                        query, key_block(name, half, KEYS, columns), (((1,), (1,)), ((), ())),
                        preferred_element_type=jnp.float32,
                    )
                    score = score.reshape(TS, COLS, PAIR) * scale + bias[r, place][None]
                    score = score.reshape(PAIR, PAIR)
                    scores[r, h, :, place * PAIR:(place + 1) * PAIR] = score
                    best = score if best is None else jnp.maximum(best, score)
                peak[r, h] = best
            return carry
        lax.fori_loop(0, heads, head, 0)

    def softmax():
        def head(h, carry):
            for r in range(2):
                most = jnp.broadcast_to(jnp.max(peak[r, h], axis=-1, keepdims=True), (PAIR, PAIR))
                summed = None
                for place in range(NPLACE):
                    part = slice(place * PAIR, (place + 1) * PAIR)
                    weight = jnp.exp(scores[r, h, :, part] - most)
                    weights[r, h, :, part] = weight.astype(jnp.bfloat16)
                    summed = weight if summed is None else summed + weight
                total[r, h] = jnp.broadcast_to(
                    1.0 / jnp.sum(summed, axis=-1, keepdims=True), (PAIR, PAIR))
            return carry
        lax.fori_loop(0, heads, head, 0)

    def add_values(*names, first=False, last=False):
        def head(h, carry):
            columns = pl.ds(pl.multiple_of(h * HD, HD), HD)
            for r in range(2):
                result = None if first else acc[r, h]
                for (name, half), place in PLACES[r].items():
                    if name not in names:
                        continue
                    part = jnp.dot(
                        weights[r, h, :, place * PAIR:(place + 1) * PAIR],
                        key_block(name, half, VALUES, columns),
                        preferred_element_type=jnp.float32,
                    )
                    result = part if result is None else result + part
                if last:
                    result = (result * total[r, h]).astype(jnp.bfloat16)
                    out[rows(r), :, columns] = result.reshape(TS, COLS, HD)
                else:
                    acc[r, h] = result
            return carry
        lax.fori_loop(0, heads, head, 0)

    left_half = lax.broadcasted_iota(jnp.int32, (TS, COLS, heads * HD), 1) < TS

    def send_corners(kind):
        from_on = left_half == (core == 0)
        for index, half in ((0, 1), (1, 0)):
            on = blocks[CORE, kind, rows(half)]
            beyond = blocks[off, kind, rows(half)]
            corner_out[index, kind] = jnp.where(from_on, on, beyond)
        start(CORNER_UP, kind, (0,))
        start(CORNER_DOWN, kind, (0,))

    get_q.wait()
    get_k.wait()
    add_keys(OWN, first=True)
    arrived(CORE, KEYS)
    add_keys(CORE)
    relay(KEYS, 0)
    start(TDIR, VALUES, (0,))
    relay(KEYS, 1)
    start(TDIR, VALUES, (1,))
    arrived(UP, KEYS)
    arrived(DOWN, KEYS)
    add_keys(UP, DOWN)
    arrived(XREL, KEYS)
    send_corners(KEYS)
    add_keys(XREL)
    relay(VALUES, 0)
    arrived(TDIR, KEYS)
    arrived(TREL, KEYS)
    add_keys(TDIR, TREL)
    arrived(CORNER_UP, KEYS, (0,))
    arrived(CORNER_DOWN, KEYS, (0,))
    add_keys(CORNER)
    relay(VALUES, 1)
    softmax()
    arrived(CORE, VALUES)
    arrived(XREL, VALUES)
    send_corners(VALUES)
    arrived(UP, VALUES)
    arrived(DOWN, VALUES)
    get_v.wait()
    add_values(OWN, CORE, XREL, UP, DOWN, first=True)
    arrived(CORNER_UP, VALUES, (0,))
    arrived(CORNER_DOWN, VALUES, (0,))
    arrived(TREL, VALUES)
    arrived(TDIR, VALUES)
    add_values(CORNER, TREL, TDIR, last=True)
    put = pltpu.make_async_copy(out, out_hbm.at[0], local_sem.at[0])
    put.start()
    for name, kind, half in started:
        when(routes[name][2], copy(name, kind, half).wait_send)
    put.wait()


def solution(mesh):
    n_az, n_lat, n_ta = mesh.shape["az"], mesh.shape["lat"], mesh.shape["ta"]

    def local(queries, keys_values, windows):
        width = queries.shape[-1]
        heads = width // HD
        vmem = pltpu.VMEM
        return pl.pallas_call(
            functools.partial(kernel, heads, n_az, n_lat, n_ta),
            out_shape=jax.ShapeDtypeStruct(queries.shape, queries.dtype),
            in_specs=[
                pl.BlockSpec(memory_space=pltpu.SMEM),
                pl.BlockSpec(memory_space=pl.ANY),
                pl.BlockSpec(memory_space=pl.ANY),
            ],
            out_specs=pl.BlockSpec(memory_space=pl.ANY),
            scratch_shapes=[
                vmem((8, 2, ROWS, COLS, width), jnp.bfloat16),
                vmem((2, 2, TS, COLS, width), jnp.bfloat16),
                vmem((2, 2, TS, COLS, width), jnp.bfloat16),
                vmem((ROWS, COLS, width), jnp.bfloat16),
                vmem((2, NPLACE, 16, PAIR), jnp.float32),
                vmem((2, heads, PAIR, NPLACE * PAIR), jnp.float32),
                vmem((2, heads, PAIR, NPLACE * PAIR), jnp.bfloat16),
                vmem((2, heads, PAIR, PAIR), jnp.float32),
                vmem((2, heads, PAIR, PAIR), jnp.float32),
                vmem((2, heads, PAIR, HD), jnp.float32),
                vmem((ROWS, COLS, width), jnp.bfloat16),
                pltpu.SemaphoreType.DMA((len(TRANSFERS), 4)),
                pltpu.SemaphoreType.DMA((len(TRANSFERS), 4)),
                pltpu.SemaphoreType.DMA((3,)),
            ],
            compiler_params=pltpu.CompilerParams(
                collective_id=0, has_side_effects=True, vmem_limit_bytes=56 * 2**20),
            name="tile_attention",
        )(windows, queries, keys_values)

    return jax.shard_map(
        local,
        mesh=mesh,
        in_specs=(
            P("ta", "lat", "az", None),
            P(None, "ta", "lat", "az", None),
            P("ta", "lat", "az", None),
        ),
        out_specs=P("ta", "lat", "az", None),
        check_vma=False,
    )
```

```python
import functools
import math

import jax
import jax.numpy as jnp
from jax import lax
from jax.experimental import pallas as pl
from jax.experimental.pallas import tpu as pltpu
from jax.sharding import PartitionSpec as P

MESH = pl.DeviceIdType.MESH
HD = 128
TS = 8
ROWS, COLS = 16, 16
PAIR = TS * COLS
NEG = -1e30

OWN, CORE, CROSS, XREL, TDIR, TREL, UP, DOWN = range(8)
CORNER_UP, CORNER_DOWN = 8, 9
PIECEWISE = (CROSS, XREL, TDIR, TREL)
TRANSFERS = (CORE, CROSS, XREL, TDIR, TREL, UP, DOWN, CORNER_UP, CORNER_DOWN)
KEYS, VALUES = 0, 1
QUARTER = ROWS // 4

CORNER = 8
PLACES = [
    {
        (OWN, 0): 0, (OWN, 1): 1, (CORE, 0): 2, (CORE, 1): 3, (XREL, 0): 4, (XREL, 1): 5,
        (UP, 0): 6, (UP, 1): 7, (DOWN, 0): 8, (CORNER, 0): 9, (TREL, 0): 10, (TDIR, 0): 11,
    },
    {
        (OWN, 0): 0, (OWN, 1): 1, (CORE, 0): 2, (CORE, 1): 3, (XREL, 0): 4, (XREL, 1): 5,
        (UP, 1): 6, (DOWN, 0): 7, (DOWN, 1): 8, (CORNER, 1): 9, (TREL, 1): 10, (TDIR, 1): 11,
    },
]
NPLACE = 12


def when(condition, action):
    if condition is None:
        action()
    else:
        pl.when(condition)(action)


def kernel(
    heads, n_az, n_lat, n_ta, windows_hbm, q_hbm, kv_hbm, out_hbm,
    blocks, corner, corner_out, q, bias, scores, weights, peak, total, acc, out,
    windows, send_sem, recv_sem, local_sem,
):
    az, lat, ta = lax.axis_index("az"), lax.axis_index("lat"), lax.axis_index("ta")
    place4 = lax.rem(az, 4)
    core = lax.rem(az, 2)
    cross = az + 3 - 2 * place4
    step = jnp.where(place4 >= 2, 1, -1)
    x_step = jnp.where(place4 == 3, -4, 4)
    outer = (place4 == 0) | (place4 == 3)
    frame_ok = lambda f: (f >= 0) & (f < n_ta)
    at = lambda a, l, t: {"az": a, "lat": l, "ta": t}
    routes = {
        CORE: (at(az + 1 - 2 * core, lat, ta),) * 2 + (None, None),
        CROSS: (at(cross, lat, ta),) * 2 + (None, None),
        XREL: (
            at(lax.rem(az + x_step + n_az, n_az), lat, ta),
            at(lax.rem(az - x_step + n_az, n_az), lat, ta),
            outer, outer,
        ),
        TDIR: (at(az, lat, ta + step), at(az, lat, ta - step), frame_ok(ta + step), frame_ok(ta - step)),
        TREL: (at(cross, lat, ta + step),) * 2 + (frame_ok(ta + step),) * 2,
        UP: (at(az, lat + 1, ta), at(az, lat - 1, ta), lat < n_lat - 1, lat > 0),
        DOWN: (at(az, lat - 1, ta), at(az, lat + 1, ta), lat > 0, lat < n_lat - 1),
    }
    routes[CORNER_UP] = routes[UP]
    routes[CORNER_DOWN] = routes[DOWN]

    barrier = pltpu.get_barrier_semaphore()
    count = 0
    for name in (CORE, CROSS, XREL, TDIR, TREL, UP, DOWN):
        _, source, sends, receives = routes[name]
        when(receives, functools.partial(
            pl.semaphore_signal, barrier, inc=1, device_id=source, device_id_type=MESH))
        count = count + (1 if sends is None else sends.astype(jnp.int32))
    pl.semaphore_wait(barrier, count)

    def rows(half):
        return pl.ds(half * TS, TS)

    def copy(name, kind, piece):
        slot = TRANSFERS.index(name)
        chunk = 4 * kind + piece
        if name in (CORNER_UP, CORNER_DOWN):
            source = corner_out.at[name - CORNER_UP, kind]
            target = corner.at[name - CORNER_UP, kind]
        else:
            part = pl.ds(piece * QUARTER, QUARTER) if name in PIECEWISE else pl.ds(0, ROWS)
            target = blocks.at[name, kind, part]
            if name in (XREL, TREL):
                source = blocks.at[CROSS, kind, part]
            else:
                source = kv_hbm.at[kind, 0, part]
        return pltpu.make_async_remote_copy(
            src_ref=source, dst_ref=target,
            send_sem=send_sem.at[slot, chunk], recv_sem=recv_sem.at[slot, chunk],
            device_id=routes[name][0], device_id_type=MESH,
        )

    started = []

    def pieces(name):
        return range(4) if name in PIECEWISE else range(1)

    def start(name, kind, some=None):
        for piece in pieces(name) if some is None else some:
            started.append((name, kind, piece))
            when(routes[name][2], copy(name, kind, piece).start)

    def arrived(name, kind, some=None):
        for piece in pieces(name) if some is None else some:
            when(routes[name][3], copy(name, kind, piece).wait_recv)

    def relay(kind, piece):
        arrived(CROSS, kind, (piece,))
        start(XREL, kind, (piece,))
        start(TREL, kind, (piece,))
        start(TDIR, kind, (piece,))

    start(CROSS, KEYS)
    start(CROSS, VALUES)
    start(UP, KEYS)
    start(DOWN, KEYS)
    start(CORE, KEYS)
    get_windows = pltpu.make_async_copy(windows_hbm, windows, local_sem.at[3])
    get_windows.start()
    get_q = pltpu.make_async_copy(q_hbm.at[0], q, local_sem.at[0])
    get_k = pltpu.make_async_copy(kv_hbm.at[KEYS, 0], blocks.at[OWN, KEYS], local_sem.at[1])
    get_v = pltpu.make_async_copy(kv_hbm.at[VALUES, 0], blocks.at[OWN, VALUES], local_sem.at[2])
    get_q.start()
    get_k.start()
    get_v.start()
    start(CORE, VALUES)
    start(UP, VALUES)
    start(DOWN, VALUES)

    def clear(name):
        def body():
            blocks[name] = jnp.zeros(blocks.shape[1:], blocks.dtype)
        return body

    def clear_corner(index):
        def body():
            corner[index] = jnp.zeros(corner.shape[1:], corner.dtype)
        return body

    for name in (TDIR, TREL, UP, DOWN):
        when(jnp.logical_not(routes[name][3]), clear(name))
    when(lat == 0, clear_corner(0))
    when(lat == n_lat - 1, clear_corner(1))

    get_windows.wait()
    rows_all, cols_all = 2 * n_lat, 2 * n_az
    lane = lax.broadcasted_iota(jnp.int32, (8, PAIR), 1)
    right_tile = lax.rem(lane // TS, 2)
    col_on = jnp.where(core == 0, 2, -2)
    for r in range(2):
        tiles = [None] * NPLACE
        for (name, half), place in PLACES[r].items():
            frame, row, col = ta, half, right_tile
            if name == CORE:
                col = col + col_on
            elif name == XREL:
                col = col - col_on
            elif name == UP:
                row = half - 2
            elif name == DOWN:
                row = half + 2
            elif name == CORNER:
                row = 3 * half - 1
                col = jnp.where(right_tile == 0, 2, -1)
            elif name == TDIR:
                frame = ta - step
            elif name == TREL:
                frame = ta + step
            row = row + 2 * lat
            there = (row >= 0) & (row < rows_all) & (frame >= 0) & (frame < n_ta)
            first = jnp.where(there, (frame * rows_all + row) * cols_all, -4 * cols_all)
            tiles[place] = first + lax.rem(col + 2 * az + cols_all, cols_all)
        tiles = jnp.stack(tiles, axis=0)
        for c in range(2):
            listed = tiles == windows[0, r, c, 0]
            for slot in range(1, windows.shape[3]):
                listed = listed | (tiles == windows[0, r, c, slot])
            bias[r, :, c * 8:(c + 1) * 8, :] = jnp.where(listed, 0.0, NEG)

    off = jnp.where(outer, XREL, CROSS)
    scale = 1.0 / math.sqrt(HD)

    def key_block(name, half, kind, columns):
        if name == CORNER:
            block = corner[half, kind, :, :, columns]
        else:
            block = blocks[off if name == XREL else name, kind, rows(half), :, columns]
        return block.reshape(PAIR, HD)

    def add_keys(*names, first=False):
        def head(h, carry):
            columns = pl.ds(pl.multiple_of(h * HD, HD), HD)
            for r in range(2):
                query = q[rows(r), :, columns].reshape(PAIR, HD)
                best = None if first else peak[r, h]
                for (name, half), place in PLACES[r].items():
                    if name not in names:
                        continue
                    score = lax.dot_general(
                        query, key_block(name, half, KEYS, columns), (((1,), (1,)), ((), ())),
                        preferred_element_type=jnp.float32,
                    )
                    score = score.reshape(TS, COLS, PAIR) * scale + bias[r, place][None]
                    score = score.reshape(PAIR, PAIR)
                    scores[r, h, :, place * PAIR:(place + 1) * PAIR] = score
                    best = score if best is None else jnp.maximum(best, score)
                peak[r, h] = best
            return carry
        lax.fori_loop(0, heads, head, 0)

    def softmax():
        def head(h, carry):
            for r in range(2):
                most = jnp.broadcast_to(jnp.max(peak[r, h], axis=-1, keepdims=True), (PAIR, PAIR))
                summed = None
                for place in range(NPLACE):
                    part = slice(place * PAIR, (place + 1) * PAIR)
                    weight = jnp.exp(scores[r, h, :, part] - most)
                    weights[r, h, :, part] = weight.astype(jnp.bfloat16)
                    summed = weight if summed is None else summed + weight
                total[r, h] = jnp.broadcast_to(
                    1.0 / jnp.sum(summed, axis=-1, keepdims=True), (PAIR, PAIR))
            return carry
        lax.fori_loop(0, heads, head, 0)

    def add_values(*names, first=False, last=False):
        def head(h, carry):
            columns = pl.ds(pl.multiple_of(h * HD, HD), HD)
            for r in range(2):
                result = None if first else acc[r, h]
                for (name, half), place in PLACES[r].items():
                    if name not in names:
                        continue
                    part = jnp.dot(
                        weights[r, h, :, place * PAIR:(place + 1) * PAIR],
                        key_block(name, half, VALUES, columns),
                        preferred_element_type=jnp.float32,
                    )
                    result = part if result is None else result + part
                if last:
                    result = (result * total[r, h]).astype(jnp.bfloat16)
                    out[rows(r), :, columns] = result.reshape(TS, COLS, HD)
                else:
                    acc[r, h] = result
            return carry
        lax.fori_loop(0, heads, head, 0)

    left_half = lax.broadcasted_iota(jnp.int32, (TS, COLS, heads * HD), 1) < TS

    def send_corners(kind):
        from_on = left_half == (core == 0)
        for index, half in ((0, 1), (1, 0)):
            on = blocks[CORE, kind, rows(half)]
            beyond = blocks[off, kind, rows(half)]
            corner_out[index, kind] = jnp.where(from_on, on, beyond)
        start(CORNER_UP, kind)
        start(CORNER_DOWN, kind)

    get_q.wait()
    get_k.wait()
    add_keys(OWN, first=True)
    relay(KEYS, 0)
    arrived(CORE, KEYS)
    add_keys(CORE)
    relay(KEYS, 1)
    relay(KEYS, 2)
    arrived(UP, KEYS)
    arrived(DOWN, KEYS)
    add_keys(UP, DOWN)
    relay(KEYS, 3)
    arrived(XREL, KEYS)
    send_corners(KEYS)
    relay(VALUES, 0)
    add_keys(XREL)
    relay(VALUES, 1)
    arrived(TREL, KEYS)
    add_keys(TREL)
    relay(VALUES, 2)
    arrived(CORNER_UP, KEYS)
    arrived(CORNER_DOWN, KEYS)
    add_keys(CORNER)
    relay(VALUES, 3)
    arrived(CORE, VALUES)
    arrived(XREL, VALUES)
    send_corners(VALUES)
    arrived(TDIR, KEYS)
    add_keys(TDIR)
    softmax()
    arrived(UP, VALUES)
    arrived(DOWN, VALUES)
    get_v.wait()
    add_values(OWN, CORE, XREL, UP, DOWN, first=True)
    arrived(CORNER_UP, VALUES)
    arrived(CORNER_DOWN, VALUES)
    arrived(TREL, VALUES)
    add_values(CORNER, TREL)
    arrived(TDIR, VALUES)
    add_values(TDIR, last=True)
    put = pltpu.make_async_copy(out, out_hbm.at[0], local_sem.at[0])
    put.start()
    for name, kind, piece in started:
        when(routes[name][2], copy(name, kind, piece).wait_send)
    put.wait()


def solution(mesh):
    n_az, n_lat, n_ta = mesh.shape["az"], mesh.shape["lat"], mesh.shape["ta"]

    def local(queries, keys_values, windows):
        width = queries.shape[-1]
        heads = width // HD
        vmem = pltpu.VMEM
        return pl.pallas_call(
            functools.partial(kernel, heads, n_az, n_lat, n_ta),
            out_shape=jax.ShapeDtypeStruct(queries.shape, queries.dtype),
            in_specs=[
                pl.BlockSpec(memory_space=pltpu.HBM),
                pl.BlockSpec(memory_space=pltpu.HBM),
                pl.BlockSpec(memory_space=pltpu.HBM),
            ],
            out_specs=pl.BlockSpec(memory_space=pl.ANY),
            scratch_shapes=[
                vmem((8, 2, ROWS, COLS, width), jnp.bfloat16),
                vmem((2, 2, TS, COLS, width), jnp.bfloat16),
                vmem((2, 2, TS, COLS, width), jnp.bfloat16),
                vmem((ROWS, COLS, width), jnp.bfloat16),
                vmem((2, NPLACE, 16, PAIR), jnp.float32),
                vmem((2, heads, PAIR, NPLACE * PAIR), jnp.float32),
                vmem((2, heads, PAIR, NPLACE * PAIR), jnp.bfloat16),
                vmem((2, heads, PAIR, PAIR), jnp.float32),
                vmem((2, heads, PAIR, PAIR), jnp.float32),
                vmem((2, heads, PAIR, HD), jnp.float32),
                vmem((ROWS, COLS, width), jnp.bfloat16),
                pltpu.SMEM(windows.shape, jnp.int32),
                pltpu.SemaphoreType.DMA((len(TRANSFERS), 8)),
                pltpu.SemaphoreType.DMA((len(TRANSFERS), 8)),
                pltpu.SemaphoreType.DMA((4,)),
            ],
            compiler_params=pltpu.CompilerParams(
                collective_id=0, has_side_effects=True, vmem_limit_bytes=56 * 2**20),
            name="tile_attention",
        )(windows, queries, keys_values)

    return jax.shard_map(
        local,
        mesh=mesh,
        in_specs=(
            P("ta", "lat", "az", None),
            P(None, "ta", "lat", "az", None),
            P("ta", "lat", "az", None),
        ),
        out_specs=P("ta", "lat", "az", None),
        check_vma=False,
    )
```

```python
import functools
import math

import jax
import jax.numpy as jnp
from jax import lax
from jax.experimental import pallas as pl
from jax.experimental.pallas import tpu as pltpu
from jax.sharding import PartitionSpec as P

MESH = pl.DeviceIdType.MESH
HD = 128
TS = 8
ROWS, COLS = 16, 16
PAIR = TS * COLS
NEG = -1e30

OWN, CORE, CROSS, XREL, TDIR, TREL, UP, DOWN = range(8)
CORNER_UP, CORNER_DOWN = 8, 9
PIECEWISE = (CROSS, XREL, TDIR, TREL)
TRANSFERS = (CORE, CROSS, XREL, TDIR, TREL, UP, DOWN, CORNER_UP, CORNER_DOWN)
KEYS, VALUES = 0, 1
FRAME_STARTS = (1, 2, 3, 4, 6, 7, 8, 8)
QUARTER = ROWS // 4

CORNER = 8
PLACES = [
    {
        (OWN, 0): 0, (OWN, 1): 1, (CORE, 0): 2, (CORE, 1): 3, (XREL, 0): 4, (XREL, 1): 5,
        (UP, 0): 6, (UP, 1): 7, (DOWN, 0): 8, (CORNER, 0): 9, (TREL, 0): 10, (TDIR, 0): 11,
    },
    {
        (OWN, 0): 0, (OWN, 1): 1, (CORE, 0): 2, (CORE, 1): 3, (XREL, 0): 4, (XREL, 1): 5,
        (UP, 1): 6, (DOWN, 0): 7, (DOWN, 1): 8, (CORNER, 1): 9, (TREL, 1): 10, (TDIR, 1): 11,
    },
]
NPLACE = 12


def when(condition, action):
    if condition is None:
        action()
    else:
        pl.when(condition)(action)


def kernel(
    heads, n_az, n_lat, n_ta, windows_hbm, q_hbm, kv_hbm, out_hbm,
    blocks, corner, corner_out, q, bias, scores, weights, peak, total, acc, out,
    windows, send_sem, recv_sem, local_sem, frame_ready,
):
    az, lat, ta = lax.axis_index("az"), lax.axis_index("lat"), lax.axis_index("ta")
    place4 = lax.rem(az, 4)
    core = lax.rem(az, 2)
    cross = az + 3 - 2 * place4
    step = jnp.where(place4 >= 2, 1, -1)
    x_step = jnp.where(place4 == 3, -4, 4)
    outer = (place4 == 0) | (place4 == 3)
    frame_ok = lambda f: (f >= 0) & (f < n_ta)
    at = lambda a, l, t: {"az": a, "lat": l, "ta": t}
    routes = {
        CORE: (at(az + 1 - 2 * core, lat, ta),) * 2 + (None, None),
        CROSS: (at(cross, lat, ta),) * 2 + (None, None),
        XREL: (
            at(lax.rem(az + x_step + n_az, n_az), lat, ta),
            at(lax.rem(az - x_step + n_az, n_az), lat, ta),
            outer, outer,
        ),
        TDIR: (at(az, lat, ta + step), at(az, lat, ta - step), frame_ok(ta + step), frame_ok(ta - step)),
        TREL: (at(cross, lat, ta + step),) * 2 + (frame_ok(ta + step),) * 2,
        UP: (at(az, lat + 1, ta), at(az, lat - 1, ta), lat < n_lat - 1, lat > 0),
        DOWN: (at(az, lat - 1, ta), at(az, lat + 1, ta), lat > 0, lat < n_lat - 1),
    }
    routes[CORNER_UP] = routes[UP]
    routes[CORNER_DOWN] = routes[DOWN]

    barrier = pltpu.get_barrier_semaphore()
    sends_frame = routes[TREL][2]
    count = 0
    for name in (CORE, CROSS, XREL, UP, DOWN, TDIR, TREL):
        _, source, sends, receives = routes[name]
        if name in (TDIR, TREL):
            source = dict(source, az=source["az"] - lax.rem(source["az"], 2) + 1)
        else:
            count = count + (1 if sends is None else sends.astype(jnp.int32))
        when(receives, functools.partial(
            pl.semaphore_signal, barrier, inc=1, device_id=source, device_id_type=MESH))
    hears = sends_frame & (core == 1)
    pl.semaphore_wait(barrier, count + jnp.where(hears, 4, 0))
    when(hears, functools.partial(
        pl.semaphore_signal, frame_ready, inc=1, device_id=routes[CORE][0], device_id_type=MESH))

    def wait_frame():
        when(sends_frame & (core == 0), functools.partial(pl.semaphore_wait, frame_ready, 1))

    def rows(half):
        return pl.ds(half * TS, TS)

    def copy(name, kind, piece):
        slot = TRANSFERS.index(name)
        chunk = 4 * kind + piece
        if name in (CORNER_UP, CORNER_DOWN):
            source = corner_out.at[name - CORNER_UP, kind]
            target = corner.at[name - CORNER_UP, kind]
        else:
            part = pl.ds(piece * QUARTER, QUARTER) if name in PIECEWISE else pl.ds(0, ROWS)
            target = blocks.at[name, kind, part]
            if name in (XREL, TREL):
                source = blocks.at[CROSS, kind, part]
            else:
                source = kv_hbm.at[kind, 0, part]
        return pltpu.make_async_remote_copy(
            src_ref=source, dst_ref=target,
            send_sem=send_sem.at[slot, chunk], recv_sem=recv_sem.at[slot, chunk],
            device_id=routes[name][0], device_id_type=MESH,
        )

    started = []

    def pieces(name):
        return range(4) if name in PIECEWISE else range(1)

    def start(name, kind, some=None):
        for piece in pieces(name) if some is None else some:
            started.append((name, kind, piece))
            when(routes[name][2], copy(name, kind, piece).start)

    def arrived(name, kind, some=None):
        for piece in pieces(name) if some is None else some:
            when(routes[name][3], copy(name, kind, piece).wait_recv)

    def send_frame(position):
        for index, where in enumerate(FRAME_STARTS):
            if where == position:
                start(TDIR, index // 4, (index % 4,))

    def relay(kind, piece):
        arrived(CROSS, kind, (piece,))
        start(XREL, kind, (piece,))
        start(TREL, kind, (piece,))
        send_frame(4 * kind + piece + 1)

    start(CROSS, KEYS)
    start(CROSS, VALUES)
    start(UP, KEYS)
    start(DOWN, KEYS)
    start(CORE, KEYS)
    get_windows = pltpu.make_async_copy(windows_hbm, windows, local_sem.at[3])
    get_windows.start()
    get_q = pltpu.make_async_copy(q_hbm.at[0], q, local_sem.at[0])
    get_k = pltpu.make_async_copy(kv_hbm.at[KEYS, 0], blocks.at[OWN, KEYS], local_sem.at[1])
    get_v = pltpu.make_async_copy(kv_hbm.at[VALUES, 0], blocks.at[OWN, VALUES], local_sem.at[2])
    get_q.start()
    get_k.start()
    get_v.start()
    start(CORE, VALUES)
    start(UP, VALUES)
    start(DOWN, VALUES)

    def clear(name):
        def body():
            blocks[name] = jnp.zeros(blocks.shape[1:], blocks.dtype)
        return body

    def clear_corner(index):
        def body():
            corner[index] = jnp.zeros(corner.shape[1:], corner.dtype)
        return body

    for name in (TDIR, TREL, UP, DOWN):
        when(jnp.logical_not(routes[name][3]), clear(name))
    when(lat == 0, clear_corner(0))
    when(lat == n_lat - 1, clear_corner(1))

    get_windows.wait()
    rows_all, cols_all = 2 * n_lat, 2 * n_az
    lane = lax.broadcasted_iota(jnp.int32, (8, PAIR), 1)
    right_tile = lax.rem(lane // TS, 2)
    col_on = jnp.where(core == 0, 2, -2)
    for r in range(2):
        tiles = [None] * NPLACE
        for (name, half), place in PLACES[r].items():
            frame, row, col = ta, half, right_tile
            if name == CORE:
                col = col + col_on
            elif name == XREL:
                col = col - col_on
            elif name == UP:
                row = half - 2
            elif name == DOWN:
                row = half + 2
            elif name == CORNER:
                row = 3 * half - 1
                col = jnp.where(right_tile == 0, 2, -1)
            elif name == TDIR:
                frame = ta - step
            elif name == TREL:
                frame = ta + step
            row = row + 2 * lat
            there = (row >= 0) & (row < rows_all) & (frame >= 0) & (frame < n_ta)
            first = jnp.where(there, (frame * rows_all + row) * cols_all, -4 * cols_all)
            tiles[place] = first + lax.rem(col + 2 * az + cols_all, cols_all)
        tiles = jnp.stack(tiles, axis=0)
        for c in range(2):
            listed = tiles == windows[0, r, c, 0]
            for slot in range(1, windows.shape[3]):
                listed = listed | (tiles == windows[0, r, c, slot])
            bias[r, :, c * 8:(c + 1) * 8, :] = jnp.where(listed, 0.0, NEG)

    off = jnp.where(outer, XREL, CROSS)
    scale = math.log2(math.e) / math.sqrt(HD)

    def key_block(name, half, kind, columns):
        if name == CORNER:
            block = corner[half, kind, :, :, columns]
        else:
            block = blocks[off if name == XREL else name, kind, rows(half), :, columns]
        return block.reshape(PAIR, HD)

    def add_keys(*names, first=False):
        def head(h, carry):
            columns = pl.ds(pl.multiple_of(h * HD, HD), HD)
            for r in range(2):
                query = q[rows(r), :, columns].reshape(PAIR, HD)
                best = None if first else peak[r, h]
                for (name, half), place in PLACES[r].items():
                    if name not in names:
                        continue
                    score = lax.dot_general(
                        query, key_block(name, half, KEYS, columns), (((1,), (1,)), ((), ())),
                        preferred_element_type=jnp.float32,
                    )
                    score = score.reshape(TS, COLS, PAIR) * scale + bias[r, place][None]
                    score = score.reshape(PAIR, PAIR)
                    scores[r, h, :, place * PAIR:(place + 1) * PAIR] = score
                    best = score if best is None else jnp.maximum(best, score)
                peak[r, h] = best
            return carry
        lax.fori_loop(0, heads, head, 0, unroll=8)

    def softmax():
        def head(h, carry):
            for r in range(2):
                most = jnp.broadcast_to(jnp.max(peak[r, h], axis=-1, keepdims=True), (PAIR, PAIR))
                summed = None
                for place in range(NPLACE):
                    part = slice(place * PAIR, (place + 1) * PAIR)
                    weight = jnp.exp2(scores[r, h, :, part] - most)
                    weights[r, h, :, part] = weight.astype(jnp.bfloat16)
                    summed = weight if summed is None else summed + weight
                total[r, h] = jnp.broadcast_to(
                    1.0 / jnp.sum(summed, axis=-1, keepdims=True), (PAIR, PAIR))
            return carry
        lax.fori_loop(0, heads, head, 0, unroll=8)

    def add_values(*names, first=False, last=False, only=(0, 1)):
        def head(h, carry):
            columns = pl.ds(pl.multiple_of(h * HD, HD), HD)
            for r in only:
                result = None if first else acc[r, h]
                for (name, half), place in PLACES[r].items():
                    if name not in names:
                        continue
                    part = jnp.dot(
                        weights[r, h, :, place * PAIR:(place + 1) * PAIR],
                        key_block(name, half, VALUES, columns),
                        preferred_element_type=jnp.float32,
                    )
                    result = part if result is None else result + part
                if last:
                    result = (result * total[r, h]).astype(jnp.bfloat16)
                    out[rows(r), :, columns] = result.reshape(TS, COLS, HD)
                else:
                    acc[r, h] = result
            return carry
        lax.fori_loop(0, heads, head, 0, unroll=8)

    left_half = lax.broadcasted_iota(jnp.int32, (TS, COLS, heads * HD), 1) < TS

    def send_corners(kind):
        from_on = left_half == (core == 0)
        for index, half in ((0, 1), (1, 0)):
            on = blocks[CORE, kind, rows(half)]
            beyond = blocks[off, kind, rows(half)]
            corner_out[index, kind] = jnp.where(from_on, on, beyond)
        start(CORNER_UP, kind)
        start(CORNER_DOWN, kind)

    get_q.wait()
    get_k.wait()
    wait_frame()
    send_frame(0)
    add_keys(OWN, first=True)
    relay(KEYS, 0)
    arrived(CORE, KEYS)
    add_keys(CORE)
    relay(KEYS, 1)
    relay(KEYS, 2)
    arrived(UP, KEYS)
    arrived(DOWN, KEYS)
    add_keys(UP, DOWN)
    relay(KEYS, 3)
    relay(VALUES, 0)
    relay(VALUES, 1)
    arrived(XREL, KEYS)
    send_corners(KEYS)
    add_keys(XREL)
    relay(VALUES, 2)
    relay(VALUES, 3)
    arrived(TDIR, KEYS)
    add_keys(TDIR)
    arrived(TREL, KEYS)
    add_keys(TREL)
    arrived(CORNER_UP, KEYS)
    arrived(CORNER_DOWN, KEYS)
    add_keys(CORNER)
    softmax()
    arrived(CORE, VALUES)
    arrived(XREL, VALUES)
    send_corners(VALUES)
    arrived(UP, VALUES)
    arrived(DOWN, VALUES)
    get_v.wait()
    add_values(OWN, CORE, XREL, UP, DOWN, first=True)
    arrived(TREL, VALUES)
    add_values(TREL)
    arrived(CORNER_UP, VALUES)
    arrived(CORNER_DOWN, VALUES)
    add_values(CORNER)
    puts = []
    for r in range(2):
        arrived(TDIR, VALUES, (2 * r, 2 * r + 1))
        add_values(TDIR, last=True, only=(r,))
        puts.append(pltpu.make_async_copy(out.at[rows(r)], out_hbm.at[0, rows(r)], local_sem.at[r]))
        puts[r].start()
    for name, kind, piece in started:
        when(routes[name][2], copy(name, kind, piece).wait_send)
    for put in puts:
        put.wait()


def solution(mesh):
    n_az, n_lat, n_ta = mesh.shape["az"], mesh.shape["lat"], mesh.shape["ta"]

    def local(queries, keys_values, windows):
        width = queries.shape[-1]
        heads = width // HD
        vmem = pltpu.VMEM
        return pl.pallas_call(
            functools.partial(kernel, heads, n_az, n_lat, n_ta),
            out_shape=jax.ShapeDtypeStruct(queries.shape, queries.dtype),
            in_specs=[
                pl.BlockSpec(memory_space=pltpu.HBM),
                pl.BlockSpec(memory_space=pltpu.HBM),
                pl.BlockSpec(memory_space=pltpu.HBM),
            ],
            out_specs=pl.BlockSpec(memory_space=pl.ANY),
            scratch_shapes=[
                vmem((8, 2, ROWS, COLS, width), jnp.bfloat16),
                vmem((2, 2, TS, COLS, width), jnp.bfloat16),
                vmem((2, 2, TS, COLS, width), jnp.bfloat16),
                vmem((ROWS, COLS, width), jnp.bfloat16),
                vmem((2, NPLACE, 16, PAIR), jnp.float32),
                vmem((2, heads, PAIR, NPLACE * PAIR), jnp.float32),
                vmem((2, heads, PAIR, NPLACE * PAIR), jnp.bfloat16),
                vmem((2, heads, PAIR, PAIR), jnp.float32),
                vmem((2, heads, PAIR, PAIR), jnp.float32),
                vmem((2, heads, PAIR, HD), jnp.float32),
                vmem((ROWS, COLS, width), jnp.bfloat16),
                pltpu.SMEM(windows.shape, jnp.int32),
                pltpu.SemaphoreType.DMA((len(TRANSFERS), 8)),
                pltpu.SemaphoreType.DMA((len(TRANSFERS), 8)),
                pltpu.SemaphoreType.DMA((4,)),
                pltpu.SemaphoreType.REGULAR,
            ],
            compiler_params=pltpu.CompilerParams(
                collective_id=0, has_side_effects=True, vmem_limit_bytes=56 * 2**20),
            name="tile_attention",
        )(windows, queries, keys_values)

    return jax.shard_map(
        local,
        mesh=mesh,
        in_specs=(
            P("ta", "lat", "az", None),
            P(None, "ta", "lat", "az", None),
            P("ta", "lat", "az", None),
        ),
        out_specs=P("ta", "lat", "az", None),
        check_vma=False,
    )
```

```python
import functools
import math

import jax
import jax.numpy as jnp
from jax import lax
from jax.experimental import pallas as pl
from jax.experimental.pallas import tpu as pltpu
from jax.sharding import PartitionSpec as P

MESH = pl.DeviceIdType.MESH
HD = 128
TS = 8
ROWS, COLS = 16, 16
PAIR = TS * COLS
NEG = -1e30

OWN, CORE, CROSS, XREL, TDIR, TREL, UP, DOWN = range(8)
CORNER_UP, CORNER_DOWN = 8, 9
PIECEWISE = (CROSS, XREL, TDIR, TREL)
TRANSFERS = (CORE, CROSS, XREL, TDIR, TREL, UP, DOWN, CORNER_UP, CORNER_DOWN)
KEYS, VALUES = 0, 1
FRAME_STARTS = (1, 2, 3, 4, 6, 7, 8, 8)
QUARTER = ROWS // 4

CORNER = 8
PLACES = [
    {
        (OWN, 0): 0, (OWN, 1): 1, (CORE, 0): 2, (CORE, 1): 3, (XREL, 0): 4, (XREL, 1): 5,
        (UP, 0): 6, (UP, 1): 7, (DOWN, 0): 8, (CORNER, 0): 9, (TREL, 0): 10, (TDIR, 0): 11,
    },
    {
        (OWN, 0): 0, (OWN, 1): 1, (CORE, 0): 2, (CORE, 1): 3, (XREL, 0): 4, (XREL, 1): 5,
        (UP, 1): 6, (DOWN, 0): 7, (DOWN, 1): 8, (CORNER, 1): 9, (TREL, 1): 10, (TDIR, 1): 11,
    },
]
NPLACE = 12


def when(condition, action):
    if condition is None:
        action()
    else:
        pl.when(condition)(action)


def kernel(
    heads, n_az, n_lat, n_ta, windows_hbm, q_hbm, kv_hbm, out,
    blocks, corner, corner_out, q, bias, scores, weights, peak, total, acc,
    windows, send_sem, recv_sem, local_sem, frame_ready,
):
    az, lat, ta = lax.axis_index("az"), lax.axis_index("lat"), lax.axis_index("ta")
    place4 = lax.rem(az, 4)
    core = lax.rem(az, 2)
    cross = az + 3 - 2 * place4
    step = jnp.where(place4 >= 2, 1, -1)
    x_step = jnp.where(place4 == 3, -4, 4)
    outer = (place4 == 0) | (place4 == 3)
    frame_ok = lambda f: (f >= 0) & (f < n_ta)
    at = lambda a, l, t: {"az": a, "lat": l, "ta": t}
    routes = {
        CORE: (at(az + 1 - 2 * core, lat, ta),) * 2 + (None, None),
        CROSS: (at(cross, lat, ta),) * 2 + (None, None),
        XREL: (
            at(lax.rem(az + x_step + n_az, n_az), lat, ta),
            at(lax.rem(az - x_step + n_az, n_az), lat, ta),
            outer, outer,
        ),
        TDIR: (at(az, lat, ta + step), at(az, lat, ta - step), frame_ok(ta + step), frame_ok(ta - step)),
        TREL: (at(cross, lat, ta + step),) * 2 + (frame_ok(ta + step),) * 2,
        UP: (at(az, lat + 1, ta), at(az, lat - 1, ta), lat < n_lat - 1, lat > 0),
        DOWN: (at(az, lat - 1, ta), at(az, lat + 1, ta), lat > 0, lat < n_lat - 1),
    }
    routes[CORNER_UP] = routes[UP]
    routes[CORNER_DOWN] = routes[DOWN]

    barrier = pltpu.get_barrier_semaphore()
    sends_frame = routes[TREL][2]
    count = 0
    for name in (CORE, CROSS, XREL, UP, DOWN, TDIR, TREL):
        _, source, sends, receives = routes[name]
        if name in (TDIR, TREL):
            source = dict(source, az=source["az"] - lax.rem(source["az"], 2) + 1)
        else:
            count = count + (1 if sends is None else sends.astype(jnp.int32))
        when(receives, functools.partial(
            pl.semaphore_signal, barrier, inc=1, device_id=source, device_id_type=MESH))
    hears = sends_frame & (core == 1)
    pl.semaphore_wait(barrier, count + jnp.where(hears, 4, 0))
    when(hears, functools.partial(
        pl.semaphore_signal, frame_ready, inc=1, device_id=routes[CORE][0], device_id_type=MESH))

    def wait_frame():
        when(sends_frame & (core == 0), functools.partial(pl.semaphore_wait, frame_ready, 1))

    def rows(half):
        return pl.ds(half * TS, TS)

    def copy(name, kind, piece):
        slot = TRANSFERS.index(name)
        chunk = 4 * kind + piece
        if name in (CORNER_UP, CORNER_DOWN):
            source = corner_out.at[name - CORNER_UP, kind]
            target = corner.at[name - CORNER_UP, kind]
        else:
            part = pl.ds(piece * QUARTER, QUARTER) if name in PIECEWISE else pl.ds(0, ROWS)
            target = blocks.at[name, kind, part]
            if name in (XREL, TREL):
                source = blocks.at[CROSS, kind, part]
            else:
                source = kv_hbm.at[kind, 0, part]
        return pltpu.make_async_remote_copy(
            src_ref=source, dst_ref=target,
            send_sem=send_sem.at[slot, chunk], recv_sem=recv_sem.at[slot, chunk],
            device_id=routes[name][0], device_id_type=MESH,
        )

    started = []

    def pieces(name):
        return range(4) if name in PIECEWISE else range(1)

    def start(name, kind, some=None):
        for piece in pieces(name) if some is None else some:
            started.append((name, kind, piece))
            when(routes[name][2], copy(name, kind, piece).start)

    def arrived(name, kind, some=None):
        for piece in pieces(name) if some is None else some:
            when(routes[name][3], copy(name, kind, piece).wait_recv)

    def send_frame(position):
        for index, where in enumerate(FRAME_STARTS):
            if where == position:
                start(TDIR, index // 4, (index % 4,))

    def relay(kind, piece):
        arrived(CROSS, kind, (piece,))
        start(XREL, kind, (piece,))
        start(TREL, kind, (piece,))
        send_frame(4 * kind + piece + 1)

    start(CROSS, KEYS)
    start(CROSS, VALUES)
    start(UP, KEYS)
    start(DOWN, KEYS)
    start(CORE, KEYS)
    get_windows = pltpu.make_async_copy(windows_hbm, windows, local_sem.at[3])
    get_windows.start()
    get_q = pltpu.make_async_copy(q_hbm.at[0], q, local_sem.at[0])
    get_k = pltpu.make_async_copy(kv_hbm.at[KEYS, 0], blocks.at[OWN, KEYS], local_sem.at[1])
    get_v = pltpu.make_async_copy(kv_hbm.at[VALUES, 0], blocks.at[OWN, VALUES], local_sem.at[2])
    get_q.start()
    get_k.start()
    get_v.start()
    start(CORE, VALUES)
    start(UP, VALUES)
    start(DOWN, VALUES)

    def clear(name):
        def body():
            blocks[name] = jnp.zeros(blocks.shape[1:], blocks.dtype)
        return body

    def clear_corner(index):
        def body():
            corner[index] = jnp.zeros(corner.shape[1:], corner.dtype)
        return body

    for name in (TDIR, TREL, UP, DOWN):
        when(jnp.logical_not(routes[name][3]), clear(name))
    when(lat == 0, clear_corner(0))
    when(lat == n_lat - 1, clear_corner(1))

    get_windows.wait()
    rows_all, cols_all = 2 * n_lat, 2 * n_az
    lane = lax.broadcasted_iota(jnp.int32, (8, PAIR), 1)
    right_tile = lax.rem(lane // TS, 2)
    col_on = jnp.where(core == 0, 2, -2)
    for r in range(2):
        tiles = [None] * NPLACE
        for (name, half), place in PLACES[r].items():
            frame, row, col = ta, half, right_tile
            if name == CORE:
                col = col + col_on
            elif name == XREL:
                col = col - col_on
            elif name == UP:
                row = half - 2
            elif name == DOWN:
                row = half + 2
            elif name == CORNER:
                row = 3 * half - 1
                col = jnp.where(right_tile == 0, 2, -1)
            elif name == TDIR:
                frame = ta - step
            elif name == TREL:
                frame = ta + step
            row = row + 2 * lat
            there = (row >= 0) & (row < rows_all) & (frame >= 0) & (frame < n_ta)
            first = jnp.where(there, (frame * rows_all + row) * cols_all, -4 * cols_all)
            tiles[place] = first + lax.rem(col + 2 * az + cols_all, cols_all)
        tiles = jnp.stack(tiles, axis=0)
        for c in range(2):
            listed = tiles == windows[0, r, c, 0]
            for slot in range(1, windows.shape[3]):
                listed = listed | (tiles == windows[0, r, c, slot])
            bias[r, :, c * 8:(c + 1) * 8, :] = jnp.where(listed, 0.0, NEG)

    off = jnp.where(outer, XREL, CROSS)
    scale = math.log2(math.e) / math.sqrt(HD)

    def key_block(name, half, kind, columns):
        if name == CORNER:
            block = corner[half, kind, :, :, columns]
        else:
            block = blocks[off if name == XREL else name, kind, rows(half), :, columns]
        return block.reshape(PAIR, HD)

    def add_keys(*names, first=False):
        def head(h, carry):
            columns = pl.ds(pl.multiple_of(h * HD, HD), HD)
            for r in range(2):
                query = q[rows(r), :, columns].reshape(PAIR, HD)
                best = None if first else peak[r, h]
                for (name, half), place in PLACES[r].items():
                    if name not in names:
                        continue
                    score = lax.dot_general(
                        query, key_block(name, half, KEYS, columns), (((1,), (1,)), ((), ())),
                        preferred_element_type=jnp.float32,
                    )
                    score = score.reshape(TS, COLS, PAIR) * scale + bias[r, place][None]
                    score = score.reshape(PAIR, PAIR)
                    scores[r, h, :, place * PAIR:(place + 1) * PAIR] = score
                    best = score if best is None else jnp.maximum(best, score)
                peak[r, h] = best
            return carry
        lax.fori_loop(0, heads, head, 0, unroll=8)

    def softmax():
        def head(h, carry):
            for r in range(2):
                most = jnp.broadcast_to(jnp.max(peak[r, h], axis=-1, keepdims=True), (PAIR, PAIR))
                summed = None
                for place in range(NPLACE):
                    part = slice(place * PAIR, (place + 1) * PAIR)
                    weight = jnp.exp2(scores[r, h, :, part] - most)
                    weights[r, h, :, part] = weight.astype(jnp.bfloat16)
                    summed = weight if summed is None else summed + weight
                total[r, h] = jnp.broadcast_to(
                    1.0 / jnp.sum(summed, axis=-1, keepdims=True), (PAIR, PAIR))
            return carry
        lax.fori_loop(0, heads, head, 0, unroll=8)

    def add_values(*names, first=False, last=False, only=(0, 1)):
        def head(h, carry):
            columns = pl.ds(pl.multiple_of(h * HD, HD), HD)
            for r in only:
                result = None if first else acc[r, h]
                for (name, half), place in PLACES[r].items():
                    if name not in names:
                        continue
                    part = jnp.dot(
                        weights[r, h, :, place * PAIR:(place + 1) * PAIR],
                        key_block(name, half, VALUES, columns),
                        preferred_element_type=jnp.float32,
                    )
                    result = part if result is None else result + part
                if last:
                    result = (result * total[r, h]).astype(jnp.bfloat16)
                    out[0, rows(r), :, columns] = result.reshape(TS, COLS, HD)
                else:
                    acc[r, h] = result
            return carry
        lax.fori_loop(0, heads, head, 0, unroll=8)

    left_half = lax.broadcasted_iota(jnp.int32, (TS, COLS, heads * HD), 1) < TS

    def send_corners(kind):
        from_on = left_half == (core == 0)
        for index, half in ((0, 1), (1, 0)):
            on = blocks[CORE, kind, rows(half)]
            beyond = blocks[off, kind, rows(half)]
            corner_out[index, kind] = jnp.where(from_on, on, beyond)
        start(CORNER_UP, kind)
        start(CORNER_DOWN, kind)

    get_q.wait()
    get_k.wait()
    wait_frame()
    send_frame(0)
    add_keys(OWN, first=True)
    relay(KEYS, 0)
    arrived(CORE, KEYS)
    add_keys(CORE)
    relay(KEYS, 1)
    relay(KEYS, 2)
    arrived(UP, KEYS)
    arrived(DOWN, KEYS)
    add_keys(UP, DOWN)
    relay(KEYS, 3)
    relay(VALUES, 0)
    relay(VALUES, 1)
    arrived(XREL, KEYS)
    send_corners(KEYS)
    add_keys(XREL)
    relay(VALUES, 2)
    relay(VALUES, 3)
    arrived(TDIR, KEYS)
    add_keys(TDIR)
    arrived(TREL, KEYS)
    add_keys(TREL)
    arrived(CORNER_UP, KEYS)
    arrived(CORNER_DOWN, KEYS)
    add_keys(CORNER)
    softmax()
    arrived(CORE, VALUES)
    arrived(XREL, VALUES)
    send_corners(VALUES)
    arrived(UP, VALUES)
    arrived(DOWN, VALUES)
    get_v.wait()
    add_values(OWN, CORE, XREL, UP, DOWN, first=True)
    arrived(TREL, VALUES)
    add_values(TREL)
    arrived(CORNER_UP, VALUES)
    arrived(CORNER_DOWN, VALUES)
    add_values(CORNER)
    for r in range(2):
        arrived(TDIR, VALUES, (2 * r, 2 * r + 1))
        add_values(TDIR, last=True, only=(r,))
    for name, kind, piece in started:
        when(routes[name][2], copy(name, kind, piece).wait_send)


def solution(mesh):
    n_az, n_lat, n_ta = mesh.shape["az"], mesh.shape["lat"], mesh.shape["ta"]

    def local(queries, keys_values, windows):
        width = queries.shape[-1]
        heads = width // HD
        vmem = pltpu.VMEM
        return pl.pallas_call(
            functools.partial(kernel, heads, n_az, n_lat, n_ta),
            out_shape=vmem(queries.shape, queries.dtype),
            in_specs=[
                pl.BlockSpec(memory_space=pltpu.HBM),
                pl.BlockSpec(memory_space=pltpu.HBM),
                pl.BlockSpec(memory_space=pltpu.HBM),
            ],
            out_specs=pl.BlockSpec(memory_space=pltpu.VMEM),
            scratch_shapes=[
                vmem((8, 2, ROWS, COLS, width), jnp.bfloat16),
                vmem((2, 2, TS, COLS, width), jnp.bfloat16),
                vmem((2, 2, TS, COLS, width), jnp.bfloat16),
                vmem((ROWS, COLS, width), jnp.bfloat16),
                vmem((2, NPLACE, 16, PAIR), jnp.float32),
                vmem((2, heads, PAIR, NPLACE * PAIR), jnp.float32),
                vmem((2, heads, PAIR, NPLACE * PAIR), jnp.bfloat16),
                vmem((2, heads, PAIR, PAIR), jnp.float32),
                vmem((2, heads, PAIR, PAIR), jnp.float32),
                vmem((2, heads, PAIR, HD), jnp.float32),
                pltpu.SMEM(windows.shape, jnp.int32),
                pltpu.SemaphoreType.DMA((len(TRANSFERS), 8)),
                pltpu.SemaphoreType.DMA((len(TRANSFERS), 8)),
                pltpu.SemaphoreType.DMA((4,)),
                pltpu.SemaphoreType.REGULAR,
            ],
            compiler_params=pltpu.CompilerParams(
                collective_id=0, has_side_effects=True, vmem_limit_bytes=40 * 2**20),
            name="tile_attention",
        )(*[pltpu.with_memory_space_constraint(x, pltpu.HBM) for x in (windows, queries, keys_values)])

    return jax.shard_map(
        local,
        mesh=mesh,
        in_specs=(
            P("ta", "lat", "az", None),
            P(None, "ta", "lat", "az", None),
            P("ta", "lat", "az", None),
        ),
        out_specs=P("ta", "lat", "az", None),
        check_vma=False,
    )
```

```python
import functools
import math

import jax
import jax.numpy as jnp
from jax import lax
from jax.experimental import pallas as pl
from jax.experimental.pallas import tpu as pltpu
from jax.sharding import PartitionSpec as P

MESH = pl.DeviceIdType.MESH
HD = 128
TS = 8
ROWS, COLS = 16, 16
PAIR = TS * COLS
NEG = -1e30

OWN, CORE, CROSS, XREL, TDIR, TREL, UP, DOWN = range(8)
CORNER_UP, CORNER_DOWN = 8, 9
PIECEWISE = (CROSS, XREL, TDIR, TREL)
TRANSFERS = (CORE, CROSS, XREL, TDIR, TREL, UP, DOWN, CORNER_UP, CORNER_DOWN)
KEYS, VALUES = 0, 1
FRAME_STARTS = (
    (0, 0, 1, 2, 5, 6, 7, 8),
    (0, 0, 3, 4, 6, 7, 8, 8),
    (1, 2, 3, 4, 6, 7, 8, 8),
)
QUARTER = ROWS // 4

CORNER = 8
PLACES = [
    {
        (OWN, 0): 0, (OWN, 1): 1, (CORE, 0): 2, (CORE, 1): 3, (XREL, 0): 4, (XREL, 1): 5,
        (UP, 0): 6, (UP, 1): 7, (DOWN, 0): 8, (CORNER, 0): 9, (TREL, 0): 10, (TDIR, 0): 11,
    },
    {
        (OWN, 0): 0, (OWN, 1): 1, (CORE, 0): 2, (CORE, 1): 3, (XREL, 0): 4, (XREL, 1): 5,
        (UP, 1): 6, (DOWN, 0): 7, (DOWN, 1): 8, (CORNER, 1): 9, (TREL, 1): 10, (TDIR, 1): 11,
    },
]
NPLACE = 12


def when(condition, action):
    if condition is None:
        action()
    else:
        pl.when(condition)(action)


def kernel(
    heads, n_az, n_lat, n_ta, windows_hbm, q_hbm, kv_hbm, out,
    blocks, corner, corner_out, q, bias, scores, weights, peak, total, acc,
    windows, send_sem, recv_sem, local_sem, frame_ready,
):
    az, lat, ta = lax.axis_index("az"), lax.axis_index("lat"), lax.axis_index("ta")
    place4 = lax.rem(az, 4)
    core = lax.rem(az, 2)
    cross = az + 3 - 2 * place4
    step = jnp.where(place4 >= 2, 1, -1)
    x_step = jnp.where(place4 == 3, -4, 4)
    outer = (place4 == 0) | (place4 == 3)
    frame_ok = lambda f: (f >= 0) & (f < n_ta)
    at = lambda a, l, t: {"az": a, "lat": l, "ta": t}
    routes = {
        CORE: (at(az + 1 - 2 * core, lat, ta),) * 2 + (None, None),
        CROSS: (at(cross, lat, ta),) * 2 + (None, None),
        XREL: (
            at(lax.rem(az + x_step + n_az, n_az), lat, ta),
            at(lax.rem(az - x_step + n_az, n_az), lat, ta),
            outer, outer,
        ),
        TDIR: (at(az, lat, ta + step), at(az, lat, ta - step), frame_ok(ta + step), frame_ok(ta - step)),
        TREL: (at(cross, lat, ta + step),) * 2 + (frame_ok(ta + step),) * 2,
        UP: (at(az, lat + 1, ta), at(az, lat - 1, ta), lat < n_lat - 1, lat > 0),
        DOWN: (at(az, lat - 1, ta), at(az, lat + 1, ta), lat > 0, lat < n_lat - 1),
    }
    routes[CORNER_UP] = routes[UP]
    routes[CORNER_DOWN] = routes[DOWN]

    barrier = pltpu.get_barrier_semaphore()
    sends_frame = routes[TREL][2]
    count = 0
    for name in (CORE, CROSS, XREL, UP, DOWN, TDIR, TREL):
        _, source, sends, receives = routes[name]
        if name in (TDIR, TREL):
            source = dict(source, az=source["az"] - lax.rem(source["az"], 2) + 1)
        else:
            count = count + (1 if sends is None else sends.astype(jnp.int32))
        when(receives, functools.partial(
            pl.semaphore_signal, barrier, inc=1, device_id=source, device_id_type=MESH))
    hears = sends_frame & (core == 1)
    pl.semaphore_wait(barrier, count + jnp.where(hears, 4, 0))
    when(hears, functools.partial(
        pl.semaphore_signal, frame_ready, inc=1, device_id=routes[CORE][0], device_id_type=MESH))

    def wait_frame():
        when(sends_frame & (core == 0), functools.partial(pl.semaphore_wait, frame_ready, 1))

    def rows(half):
        return pl.ds(half * TS, TS)

    def copy(name, kind, piece):
        slot = TRANSFERS.index(name)
        chunk = 4 * kind + piece
        if name in (CORNER_UP, CORNER_DOWN):
            source = corner_out.at[name - CORNER_UP, kind]
            target = corner.at[name - CORNER_UP, kind]
        else:
            part = pl.ds(piece * QUARTER, QUARTER) if name in PIECEWISE else pl.ds(0, ROWS)
            target = blocks.at[name, kind, part]
            if name in (XREL, TREL):
                source = blocks.at[CROSS, kind, part]
            else:
                source = kv_hbm.at[kind, 0, part]
        return pltpu.make_async_remote_copy(
            src_ref=source, dst_ref=target,
            send_sem=send_sem.at[slot, chunk], recv_sem=recv_sem.at[slot, chunk],
            device_id=routes[name][0], device_id_type=MESH,
        )

    started = []

    def pieces(name):
        return range(4) if name in PIECEWISE else range(1)

    def start(name, kind, some=None):
        for piece in pieces(name) if some is None else some:
            started.append((name, kind, piece))
            when(routes[name][2], copy(name, kind, piece).start)

    def arrived(name, kind, some=None):
        for piece in pieces(name) if some is None else some:
            when(routes[name][3], copy(name, kind, piece).wait_recv)

    lower = (step < 0) & (ta < n_ta - 2)
    next_to_last = (step < 0) & (ta == n_ta - 2)
    others = jnp.logical_not(lower | next_to_last)

    def send_frame(position):
        for index in range(8):
            kind, piece = index // 4, index % 4
            chosen = [
                group for group, starts in zip((lower, next_to_last, others), FRAME_STARTS)
                if starts[index] == position
            ]
            if chosen:
                sends = routes[TDIR][2] & functools.reduce(jnp.logical_or, chosen)
                pl.when(sends)(copy(TDIR, kind, piece).start)
            if position == 8:
                started.append((TDIR, kind, piece))

    def relay(kind, piece):
        arrived(CROSS, kind, (piece,))
        start(XREL, kind, (piece,))
        start(TREL, kind, (piece,))
        send_frame(4 * kind + piece + 1)

    start(CROSS, KEYS)
    start(CROSS, VALUES)
    start(UP, KEYS)
    start(DOWN, KEYS)
    start(CORE, KEYS)
    get_windows = pltpu.make_async_copy(windows_hbm, windows, local_sem.at[3])
    get_windows.start()
    get_q = pltpu.make_async_copy(q_hbm.at[0], q, local_sem.at[0])
    get_k = pltpu.make_async_copy(kv_hbm.at[KEYS, 0], blocks.at[OWN, KEYS], local_sem.at[1])
    get_v = pltpu.make_async_copy(kv_hbm.at[VALUES, 0], blocks.at[OWN, VALUES], local_sem.at[2])
    get_q.start()
    get_k.start()
    get_v.start()
    start(CORE, VALUES)
    start(UP, VALUES)
    start(DOWN, VALUES)

    def clear(name):
        def body():
            blocks[name] = jnp.zeros(blocks.shape[1:], blocks.dtype)
        return body

    def clear_corner(index):
        def body():
            corner[index] = jnp.zeros(corner.shape[1:], corner.dtype)
        return body

    for name in (TDIR, TREL, UP, DOWN):
        when(jnp.logical_not(routes[name][3]), clear(name))
    when(lat == 0, clear_corner(0))
    when(lat == n_lat - 1, clear_corner(1))

    get_windows.wait()
    rows_all, cols_all = 2 * n_lat, 2 * n_az
    lane = lax.broadcasted_iota(jnp.int32, (8, PAIR), 1)
    right_tile = lax.rem(lane // TS, 2)
    col_on = jnp.where(core == 0, 2, -2)
    for r in range(2):
        tiles = [None] * NPLACE
        for (name, half), place in PLACES[r].items():
            frame, row, col = ta, half, right_tile
            if name == CORE:
                col = col + col_on
            elif name == XREL:
                col = col - col_on
            elif name == UP:
                row = half - 2
            elif name == DOWN:
                row = half + 2
            elif name == CORNER:
                row = 3 * half - 1
                col = jnp.where(right_tile == 0, 2, -1)
            elif name == TDIR:
                frame = ta - step
            elif name == TREL:
                frame = ta + step
            row = row + 2 * lat
            there = (row >= 0) & (row < rows_all) & (frame >= 0) & (frame < n_ta)
            first = jnp.where(there, (frame * rows_all + row) * cols_all, -4 * cols_all)
            tiles[place] = first + lax.rem(col + 2 * az + cols_all, cols_all)
        tiles = jnp.stack(tiles, axis=0)
        for c in range(2):
            listed = tiles == windows[0, r, c, 0]
            for slot in range(1, windows.shape[3]):
                listed = listed | (tiles == windows[0, r, c, slot])
            bias[r, :, c * 8:(c + 1) * 8, :] = jnp.where(listed, 0.0, NEG)

    off = jnp.where(outer, XREL, CROSS)
    scale = math.log2(math.e) / math.sqrt(HD)

    def key_block(name, half, kind, columns):
        if name == CORNER:
            block = corner[half, kind, :, :, columns]
        else:
            block = blocks[off if name == XREL else name, kind, rows(half), :, columns]
        return block.reshape(PAIR, HD)

    def add_keys(*names, first=False):
        def head(h, carry):
            columns = pl.ds(pl.multiple_of(h * HD, HD), HD)
            for r in range(2):
                query = q[rows(r), :, columns].reshape(PAIR, HD)
                best = None if first else peak[r, h]
                for (name, half), place in PLACES[r].items():
                    if name not in names:
                        continue
                    score = lax.dot_general(
                        query, key_block(name, half, KEYS, columns), (((1,), (1,)), ((), ())),
                        preferred_element_type=jnp.float32,
                    )
                    score = score.reshape(TS, COLS, PAIR) * scale + bias[r, place][None]
                    score = score.reshape(PAIR, PAIR)
                    scores[r, h, :, place * PAIR:(place + 1) * PAIR] = score
                    best = score if best is None else jnp.maximum(best, score)
                peak[r, h] = best
            return carry
        lax.fori_loop(0, heads, head, 0, unroll=8)

    def softmax():
        def head(h, carry):
            for r in range(2):
                most = jnp.broadcast_to(jnp.max(peak[r, h], axis=-1, keepdims=True), (PAIR, PAIR))
                summed = None
                for place in range(NPLACE):
                    part = slice(place * PAIR, (place + 1) * PAIR)
                    weight = jnp.exp2(scores[r, h, :, part] - most)
                    weights[r, h, :, part] = weight.astype(jnp.bfloat16)
                    summed = weight if summed is None else summed + weight
                total[r, h] = jnp.broadcast_to(
                    1.0 / jnp.sum(summed, axis=-1, keepdims=True), (PAIR, PAIR))
            return carry
        lax.fori_loop(0, heads, head, 0, unroll=8)

    def add_values(*names, first=False, last=False, only=(0, 1)):
        def head(h, carry):
            columns = pl.ds(pl.multiple_of(h * HD, HD), HD)
            for r in only:
                result = None if first else acc[r, h]
                for (name, half), place in PLACES[r].items():
                    if name not in names:
                        continue
                    part = jnp.dot(
                        weights[r, h, :, place * PAIR:(place + 1) * PAIR],
                        key_block(name, half, VALUES, columns),
                        preferred_element_type=jnp.float32,
                    )
                    result = part if result is None else result + part
                if last:
                    result = (result * total[r, h]).astype(jnp.bfloat16)
                    out[0, rows(r), :, columns] = result.reshape(TS, COLS, HD)
                else:
                    acc[r, h] = result
            return carry
        lax.fori_loop(0, heads, head, 0, unroll=8)

    left_half = lax.broadcasted_iota(jnp.int32, (TS, COLS, heads * HD), 1) < TS

    def send_corners(kind):
        from_on = left_half == (core == 0)
        for index, half in ((0, 1), (1, 0)):
            on = blocks[CORE, kind, rows(half)]
            beyond = blocks[off, kind, rows(half)]
            corner_out[index, kind] = jnp.where(from_on, on, beyond)
        start(CORNER_UP, kind)
        start(CORNER_DOWN, kind)

    get_q.wait()
    get_k.wait()
    wait_frame()
    send_frame(0)
    add_keys(OWN, first=True)
    relay(KEYS, 0)
    arrived(CORE, KEYS)
    add_keys(CORE)
    relay(KEYS, 1)
    relay(KEYS, 2)
    arrived(UP, KEYS)
    arrived(DOWN, KEYS)
    add_keys(UP, DOWN)
    relay(KEYS, 3)
    relay(VALUES, 0)
    relay(VALUES, 1)
    arrived(XREL, KEYS)
    send_corners(KEYS)
    add_keys(XREL)
    relay(VALUES, 2)
    relay(VALUES, 3)
    arrived(TDIR, KEYS)
    add_keys(TDIR)
    arrived(TREL, KEYS)
    add_keys(TREL)
    arrived(CORNER_UP, KEYS)
    arrived(CORNER_DOWN, KEYS)
    add_keys(CORNER)
    softmax()
    arrived(CORE, VALUES)
    arrived(XREL, VALUES)
    send_corners(VALUES)
    arrived(UP, VALUES)
    arrived(DOWN, VALUES)
    get_v.wait()
    add_values(OWN, CORE, XREL, UP, DOWN, first=True)
    arrived(TREL, VALUES)
    add_values(TREL)
    arrived(CORNER_UP, VALUES)
    arrived(CORNER_DOWN, VALUES)
    add_values(CORNER)
    for r in range(2):
        arrived(TDIR, VALUES, (2 * r, 2 * r + 1))
        add_values(TDIR, last=True, only=(r,))
    for name, kind, piece in started:
        when(routes[name][2], copy(name, kind, piece).wait_send)


def solution(mesh):
    n_az, n_lat, n_ta = mesh.shape["az"], mesh.shape["lat"], mesh.shape["ta"]

    def local(queries, keys_values, windows):
        width = queries.shape[-1]
        heads = width // HD
        vmem = pltpu.VMEM
        return pl.pallas_call(
            functools.partial(kernel, heads, n_az, n_lat, n_ta),
            out_shape=vmem(queries.shape, queries.dtype),
            in_specs=[
                pl.BlockSpec(memory_space=pltpu.HBM),
                pl.BlockSpec(memory_space=pltpu.HBM),
                pl.BlockSpec(memory_space=pltpu.HBM),
            ],
            out_specs=pl.BlockSpec(memory_space=pltpu.VMEM),
            scratch_shapes=[
                vmem((8, 2, ROWS, COLS, width), jnp.bfloat16),
                vmem((2, 2, TS, COLS, width), jnp.bfloat16),
                vmem((2, 2, TS, COLS, width), jnp.bfloat16),
                vmem((ROWS, COLS, width), jnp.bfloat16),
                vmem((2, NPLACE, 16, PAIR), jnp.float32),
                vmem((2, heads, PAIR, NPLACE * PAIR), jnp.float32),
                vmem((2, heads, PAIR, NPLACE * PAIR), jnp.bfloat16),
                vmem((2, heads, PAIR, PAIR), jnp.float32),
                vmem((2, heads, PAIR, PAIR), jnp.float32),
                vmem((2, heads, PAIR, HD), jnp.float32),
                pltpu.SMEM(windows.shape, jnp.int32),
                pltpu.SemaphoreType.DMA((len(TRANSFERS), 8)),
                pltpu.SemaphoreType.DMA((len(TRANSFERS), 8)),
                pltpu.SemaphoreType.DMA((4,)),
                pltpu.SemaphoreType.REGULAR,
            ],
            compiler_params=pltpu.CompilerParams(
                collective_id=0, has_side_effects=True, vmem_limit_bytes=40 * 2**20),
            name="tile_attention",
        )(*[pltpu.with_memory_space_constraint(x, pltpu.HBM) for x in (windows, queries, keys_values)])

    return jax.shard_map(
        local,
        mesh=mesh,
        in_specs=(
            P("ta", "lat", "az", None),
            P(None, "ta", "lat", "az", None),
            P("ta", "lat", "az", None),
        ),
        out_specs=P("ta", "lat", "az", None),
        check_vma=False,
    )
```
